128 devices in a mesh: dp: 16 (over y, z_lo, core), mp: 8 (over x, z_hi).
Axes of the slice: x: 4, y: 4, z: 4 (z_hi: 2, z_lo: 2; z = z_hi * 2 + z_lo), core: 2. Of those that a mesh axis runs over, the one named last changes fastest.
Arguments:
- layer_input: bfloat16 [16384, 8192], P(('dp', 'mp'))
- norm_gain: float32 [8192], replicated, may hold values from 0.5 to 1.5
- query_weight: bfloat16 [8192, 4096], P(None, 'mp'), may hold values from -0.0625 to 0.0625
- key_weight: bfloat16 [8192, 1024], P(None, 'mp'), may hold values from -0.0625 to 0.0625
- value_weight: bfloat16 [8192, 1024], P(None, 'mp'), may hold values from -0.0625 to 0.0625
- query_grad: bfloat16 [16384, 4096], P('dp', 'mp'), may hold values from -12 to 12
- key_grad: bfloat16 [16384, 1024], P('dp', 'mp'), may hold values from -12 to 12
- value_grad: bfloat16 [16384, 1024], P('dp', 'mp'), may hold values from -12 to 12
- positions: int32 [16384], P('dp'), may hold values from 0 to 1022, as said below
Outputs:
- input_grad: bfloat16 [16384, 8192], P(('dp', 'mp'))
- key_weight_grad: float32 [8192, 1024], P('dp', 'mp')
- value_weight_grad: float32 [8192, 1024], P('dp', 'mp')
- query_weight_grad: float32 [8192, 4096], P('dp', 'mp')
The draws below stay inside these ranges and needn't reach their ends.
Inputs may be any that keep to these rules, and one draw needn't show every extreme that they name: Each slab of 1024 consecutive tokens holds a prompt at positions 0 upward, then a first completion continuing from the prompt's end, then a second completion that restarts at the prompt's end.
All inputs are finite; a program needn't handle non-finite values.
Results may differ from the reference program's by a relative error of at most 0.023.
Values may be sent and summed in bfloat16 or wider, within the bound.
A program may use at most 192 MiB of HBM per device.

```python
import math
import jax
import jax.numpy as jnp
from jax import lax

D = 8192
KVH = 8
HD = 128
QH = 32
SLAB = 1024
TOKENS = 16384
N_DP = 16
N_MP = 8


def draw_layer_input(key, part):
    first, second, third = jax.random.split(jax.random.fold_in(key, 11), 3)
    row_scale = jnp.exp(jax.random.uniform(first, (TOKENS, 1), jnp.float32, 0.0, 2.3))
    col_scale = jnp.exp(jax.random.uniform(second, (1, D), jnp.float32, -1.15, 1.15))
    base = jax.random.normal(third, (TOKENS, D), jnp.float32)
    return (base * row_scale * col_scale).astype(jnp.bfloat16)


def draw_positions(key, part):
    groups = TOKENS // SLAB
    first, second = jax.random.split(jax.random.fold_in(key, 23), 2)
    prompt = jax.random.randint(first, (groups, 1), SLAB // 8, SLAB // 2 + 1)
    spread = jax.random.randint(second, (groups, 1), 0, 1048576)
    opening = 1 + spread % (SLAB - prompt - 1)
    slab_index = jnp.arange(groups, dtype=jnp.int32)[:, None]
    opening = jnp.where(slab_index == 0, 1, opening)
    index = jnp.arange(SLAB, dtype=jnp.int32)[None, :]
    place = jnp.where(index < prompt + opening, index, index - opening)
    return place.reshape(TOKENS).astype(jnp.int32)


def level_of(stream_key, extent, cuts, least, top_value):
    def one(dim, blocks):
        steps = jax.random.uniform(jax.random.fold_in(jax.random.fold_in(stream_key, 6), dim), (blocks,), jnp.float32, least / len(cuts), top_value / len(cuts))
        return jnp.repeat(jnp.exp(steps), extent[dim] // blocks).reshape((-1,) + (1,) * (len(extent) - dim - 1))

    level = one(*cuts[0])
    for cut in cuts[1:]:
        level = level * one(*cut)
    return level


def noise(stream_key, extent, deviation, reach, shards=(), kind=jnp.bfloat16):
    result = jax.random.normal(stream_key, extent, jnp.float32) * deviation
    if len(shards) > 0:
        result = level_of(stream_key, extent, shards, -0.22, 0.18) * result
    return jnp.clip(result, min=-reach, max=reach).astype(kind)


def setup_inputs(seed: int = 0) -> dict:
    key_of = jax.random.split(jax.random.key(seed), 10)
    return {
        "layer_input": draw_layer_input(jax.random.fold_in(key_of[9], 71), 0),
        "norm_gain": jnp.clip(1.0 + 0.1 * jax.random.normal(key_of[1], (D,), jnp.float32), 0.5, 1.5),
        "query_weight": noise(key_of[2], (D, QH * HD), D ** -0.5, 0.0625, ((1, 8),)),
        "key_weight": noise(key_of[3], (D, KVH * HD), D ** -0.5, 0.0625, ((1, 8),)),
        "value_weight": noise(key_of[4], (D, KVH * HD), D ** -0.5, 0.0625, ((1, 8),)),
        "query_grad": noise(key_of[5], (TOKENS, QH * HD), 2.0, 12.0, ((0, 16), (1, 8))),
        "key_grad": noise(key_of[6], (TOKENS, KVH * HD), 2.0, 12.0, ((0, 16), (1, 8))),
        "value_grad": noise(key_of[7], (TOKENS, KVH * HD), 2.0, 12.0, ((0, 16), (1, 8))),
        "positions": draw_positions(jax.random.fold_in(key_of[9], 71), 0),
    }


def normalize(rows, norm_gain):
    value_rows = rows.astype(jnp.float32)
    inverse_deviation = lax.rsqrt(lax.optimization_barrier(jnp.mean(value_rows * value_rows, axis=-1, keepdims=True)) + 1e-05)
    normed = (value_rows * inverse_deviation * norm_gain.astype(jnp.float32)).astype(jnp.bfloat16)
    return (normed, inverse_deviation)

def rope_back(grad, positions):
    count, width = grad.shape
    half = HD // 2
    value_rows = grad.astype(jnp.float32).reshape(count, width // HD, HD)
    index = jnp.arange(half, dtype=jnp.float32)
    freq = jnp.exp(-(2.0 * index / HD) * jnp.log(10000.0))
    angle = positions.astype(jnp.float32)[:, None] * freq[None, :]
    cosine = jnp.cos(angle)[:, None, :]
    sine = jnp.sin(angle)[:, None, :]
    first = value_rows[..., :half]
    second = value_rows[..., half:]
    back = jnp.concatenate([first * cosine + second * sine, second * cosine - first * sine], axis=-1)
    return back.reshape(count, width).astype(jnp.bfloat16)

def tgrad(normed, cot):
    return lax.dot_general(normed, cot, (((0,), (0,)), ((), ())), preferred_element_type=jnp.float32)

def reference(layer_input, norm_gain, query_weight, key_weight, value_weight, query_grad, key_grad, value_grad, positions):
    width = KVH * HD
    qwidth = QH * HD
    group_cols = width // N_MP
    qgroup_cols = qwidth // N_MP
    gain = norm_gain.astype(jnp.float32)

    def one_slab(carry, slab_index):
        start = (slab_index * SLAB).astype(jnp.int32)
        rows = lax.dynamic_slice_in_dim(layer_input, start, SLAB, 0)
        qgrad = lax.dynamic_slice_in_dim(query_grad, start, SLAB, 0)
        kgrad = lax.dynamic_slice_in_dim(key_grad, start, SLAB, 0)
        vgrad = lax.dynamic_slice_in_dim(value_grad, start, SLAB, 0)
        where = lax.dynamic_slice_in_dim(positions, start, SLAB, 0)
        normed, inverse_deviation = normalize(rows, norm_gain)
        key_backward_grad = rope_back(kgrad, where)
        query_back = rope_back(qgrad, where)
        key_acc = carry[0] + tgrad(normed, key_backward_grad)
        value_acc = carry[1] + tgrad(normed, vgrad)
        query_acc = carry[2] + tgrad(normed, query_back)
        normed_grad = jnp.zeros((SLAB, D), jnp.float32)
        for group in range(N_MP):
            low = group * group_cols
            qlow = group * qgroup_cols
            cot = jnp.concatenate([query_back[:, qlow:qlow + qgroup_cols], key_backward_grad[:, low:low + group_cols], vgrad[:, low:low + group_cols]], axis=1)
            mats = jnp.concatenate([query_weight[:, qlow:qlow + qgroup_cols], key_weight[:, low:low + group_cols], value_weight[:, low:low + group_cols]], axis=1)
            part = lax.dot_general(cot, mats, (((1,), (1,)), ((), ())), preferred_element_type=jnp.float32)
            part = lax.optimization_barrier(part.astype(jnp.bfloat16))
            normed_grad = normed_grad + part.astype(jnp.float32)
        value_rows = rows.astype(jnp.float32)
        gain_scaled_rows = normed_grad * gain
        centered_input_unit = value_rows * inverse_deviation
        backward_result = inverse_deviation * (gain_scaled_rows - centered_input_unit * lax.optimization_barrier(jnp.mean(centered_input_unit * gain_scaled_rows, axis=-1, keepdims=True)))
        return ((key_acc, value_acc, query_acc), backward_result.astype(jnp.bfloat16))
    init = (jnp.zeros((D, width), jnp.float32), jnp.zeros((D, width), jnp.float32), jnp.zeros((D, qwidth), jnp.float32))
    sums, grads = lax.scan(one_slab, init, jnp.arange(N_DP, dtype=jnp.int32))
    factor = 1.0 / math.sqrt(TOKENS)
    input_grad = grads.reshape(TOKENS, D)
    return (input_grad, sums[0] * factor, sums[1] * factor, sums[2] * factor)
```

```python
import functools
import math

import jax
import jax.numpy as jnp
from jax import lax
from jax.experimental import pallas as pl
from jax.experimental.pallas import tpu as pltpu
from jax.sharding import PartitionSpec as P

HD = 128
NY, NX = 4, 4
HOPS = (1, 3, 2)
BF = jnp.bfloat16
F32 = jnp.float32
MESH = pl.DeviceIdType.MESH


def mult(value, by):
    return pl.multiple_of(value, by)


def core_kernel(
    x_ref, gain_ref, wq_ref, wk_ref, wv_ref, q_ref, k_ref, v_ref, pos_ref, freq_ref,
    dxs_ref, dws_ref,
    nt, xst, cot, wb, coresend, corerecv, sum2, yrecv, zlsend, zlrecv, xsend, dxsend, dxrecv, dxown,
    w_s, w_r, wl_s, wy_s, wy_r, wc_s, wc_r, x_s, x_r, xl_s, xz_s, xz_r, c_s, c_r,
    pc_s, pc_r, py_s, py_r, pz_s, pz_r, px_s, px_r, pl_s, dz_s, dz_r, da_s, da_r, dl_s,
):
    dp = lax.axis_index("dp")
    mp = lax.axis_index("mp")
    y, zl, core = dp // 4, (dp // 2) % 2, dp % 2
    x, zh = mp // 2, mp % 2

    def at(y=y, zl=zl, core=core, x=x, zh=zh):
        return (y * 4 + zl * 2 + core, x * 2 + zh)

    def hop(v, k):
        return lax.rem(v + k, 4)

    def remote(src, dst, ssem, rsem, where):
        return pltpu.make_async_remote_copy(
            src_ref=src, dst_ref=dst, send_sem=ssem, recv_sem=rsem,
            device_id=where, device_id_type=MESH,
        )

    peers = [at(x=hop(x, k)) for k in HOPS] + [at(y=hop(y, k)) for k in HOPS]
    peers += [at(zl=1 - zl), at(zh=1 - zh), at(core=1 - core)]
    barrier = pltpu.get_barrier_semaphore()
    for peer in peers:
        pl.semaphore_signal(barrier, inc=1, device_id=peer, device_id_type=MESH)
    pl.semaphore_wait(barrier, len(peers))

    own_rows = core * 8 + y * 2
    widths = ((wq_ref, 0, 512), (wk_ref, 512, 128), (wv_ref, 640, 128))

    def w_part(j, to_x):
        ref, low, width = widths[j]
        src = ref.at[y, :, core, to_x]
        dst = wb.at[pl.ds(own_rows, 2), :, pl.ds(mult(x * 768 + low, 128), width)]
        return src, dst

    w_copies = []
    for i, k in enumerate(HOPS):
        for j in range(3):
            src, dst = w_part(j, hop(x, k))
            copy = remote(src, dst, w_s.at[i, j], w_r.at[i, j], at(x=hop(x, k)))
            copy.start()
            w_copies.append(copy)
    w_local = []
    for j in range(3):
        src, dst = w_part(j, x)
        copy = pltpu.make_async_copy(src, dst, wl_s.at[j])
        copy.start()
        w_local.append(copy)

    def squares(c, total):
        piece = x_ref[:, pl.ds(mult(c * 512, 512), 512)].astype(F32)
        piece = piece * piece
        return total + (piece[:, :128] + piece[:, 128:256]) + (piece[:, 256:384] + piece[:, 384:])

    total = lax.fori_loop(0, 16, squares, jnp.zeros((128, 128), F32))
    mean = jnp.sum(total, axis=1, keepdims=True) * (1.0 / 8192)
    rstd = lax.rsqrt(mean + 1e-05)

    def x_to(to_x):
        def block(kappa, carry):
            c, yy, zz = kappa // 8, (kappa // 2) % 4, kappa % 2
            low = mult((yy * 4 + zz * 2 + c) * 512 + to_x * 128, 128)
            rows = x_ref[:, pl.ds(low, 128)].astype(F32)
            normed = rows * rstd * gain_ref[:, pl.ds(low, 128)]
            nt[to_x, kappa] = normed.T.astype(BF)
            return carry

        lax.fori_loop(0, 16, block, 0)

    x_slot = pl.ds(mult((zh * 4 + x) * 128, 128), 128)
    x_copies = []
    for i, k in enumerate(HOPS):
        to_x = hop(x, k)
        x_to(to_x)
        copy = remote(nt.at[to_x], xst.at[:, :, x_slot], x_s.at[i], x_r.at[i], at(x=to_x))
        copy.start()
        x_copies.append(copy)
    x_to(x)
    x_local = pltpu.make_async_copy(nt.at[x], xst.at[:, :, x_slot], xl_s)
    x_local.start()

    def x_forward(i, from_x):
        slot = pl.ds(mult((zh * 4 + from_x) * 128, 128), 128)
        copy = remote(xst.at[:, :, slot], xst.at[:, :, slot], xz_s.at[i], xz_r.at[i], at(zh=1 - zh))
        copy.start()
        return copy

    x_local.wait()
    xz_copies = [x_forward(3, x)]

    lane = lax.broadcasted_iota(jnp.int32, (128, 128), 1)

    def rope(t, carry):
        block = (t % 4) * 2 + t // 4
        rows = pl.ds(mult(block * 128, 128), 128)
        place = jnp.broadcast_to(pos_ref[pl.ds(block, 1), :].astype(F32), (128, 128)).T
        angle = place * freq_ref[...]
        cosine = jnp.cos(angle)
        sine = jnp.sin(angle)
        sine = jnp.where(lane < 64, sine, -sine)
        out = pl.ds(mult(t * 128, 128), 128)
        for h in range(5):
            v = q_ref[rows, pl.ds(h * 128, 128)] if h < 4 else k_ref[rows, :]
            v = v.astype(F32)
            back = v * cosine + pltpu.roll(v, 64, 1) * sine
            cot[out, pl.ds(mult(x * 768 + h * 128, 128), 128)] = back.astype(BF)
        cot[out, pl.ds(mult(x * 768 + 640, 128), 128)] = v_ref[rows, :]
        return carry

    lax.fori_loop(0, 8, rope, 0)

    for copy in w_local:
        copy.wait()
    for copy in w_copies:
        copy.wait_recv()
    mine = wb.at[pl.ds(own_rows, 2)]
    wy_copies = []
    for i, k in enumerate(HOPS):
        copy = remote(mine, mine, wy_s.at[i], wy_r.at[i], at(y=hop(y, k)))
        copy.start()
        wy_copies.append(copy)

    def w_core(i, from_y):
        rows = wb.at[pl.ds(core * 8 + from_y * 2, 2)]
        copy = remote(rows, rows, wc_s.at[i], wc_r.at[i], at(core=1 - core))
        copy.start()
        return copy

    wc_copies = [w_core(3, y)]
    for i, k in enumerate(HOPS):
        x_copies[i].wait_recv()
        xz_copies.append(x_forward(i, hop(x, 4 - k)))

    def cot_copy(i, row, rows):
        part = cot.at[pl.ds(mult(row, 512), rows), pl.ds(mult(x * 768, 128), 768)]
        return part

    c_copies = []
    for i in range(2):
        part = cot_copy(i, 0, 1024)
        copy = remote(part, part, c_s.at[i], c_r.at[i], at(x=hop(x, HOPS[i])))
        copy.start()
        c_copies.append(copy)

    for i, k in enumerate(HOPS):
        wy_copies[i].wait_recv()
        wc_copies.append(w_core(i, hop(y, 4 - k)))
    for copy in xz_copies:
        copy.wait_recv()

    blocks = (x, hop(x, 3), hop(x, 1), hop(x, 2))

    def wdot(kappa, b):
        return jnp.dot(
            xst[pl.ds(kappa, 2)].reshape(256, 1024),
            cot[:, pl.ds(mult(b * 768, 128), 768)],
            preferred_element_type=F32,
        )

    def pc_copy(r, k):
        return remote(coresend.at[r % 2, k], corerecv.at[r, k], pc_s.at[r, k], pc_r.at[r, k], at(core=1 - core))

    def py_copy(r, k):
        return remote(sum2.at[r, k], yrecv.at[r, k], py_s.at[r, k], py_r.at[r, k], at(y=hop(y, 1 + k)))

    def pz_copy(r):
        return remote(zlsend.at[r], zlrecv.at[r], pz_s.at[r], pz_r.at[r], at(zl=1 - zl))

    def px_copy(r):
        if r == 0:
            return pltpu.make_async_copy(xsend.at[r], dws_ref.at[x], pl_s)
        return remote(xsend.at[r], dws_ref.at[x], px_s.at[r - 1], px_r.at[r - 1], at(x=blocks[r]))

    def wgrad(r):
        b = blocks[r]

        def other(k, carry):
            if r >= 2:
                pc_copy(r - 2, k).wait_send()
            coresend[r % 2, k] = wdot((1 - core) * 8 + hop(y, 1 + k) * 2, b).astype(BF)
            pc_copy(r, k).start()
            return carry

        lax.fori_loop(0, 4, other, 0)

        def own(k, carry):
            part = wdot(core * 8 + hop(y, 1 + k) * 2, b)
            pc_copy(r, k).wait_recv()
            sum2[r, k] = (part + corerecv[r, k].astype(F32)).astype(BF)

            @pl.when(k < 3)
            def _():
                py_copy(r, k).start()

            return carry

        lax.fori_loop(0, 4, own, 0)

    def y_total(r, low):
        rows = pl.ds(mult(low * 128, 128), 128)
        return (
            (sum2[r, 3, rows, :].astype(F32) + yrecv[r, 0, rows, :].astype(F32))
            + (yrecv[r, 1, rows, :].astype(F32) + yrecv[r, 2, rows, :].astype(F32))
        )

    def stage_a(r):
        for k in range(3):
            py_copy(r, k).wait_recv()
        zlsend[r] = y_total(r, 1 - zl).astype(BF)
        pz_copy(r).start()

    def stage_b(r):
        pz_copy(r).wait_recv()
        xsend[r] = (y_total(r, zl) + zlrecv[r].astype(F32)).astype(BF)
        px_copy(r).start()

    def ddot(half, n):
        return lax.dot_general(
            cot[pl.ds(mult(half * 512, 512), 512), :],
            wb[pl.ds(n * 2, 2)].reshape(256, 3072),
            (((1,), (1,)), ((), ())),
            preferred_element_type=F32,
        )

    def dz_copy(n):
        return remote(dxsend.at[n], dxrecv.at[n], dz_s.at[n], dz_r.at[n], at(zh=1 - zh))

    def da_copy(n, i):
        to_x = hop(x, HOPS[i])
        return remote(
            dxown.at[n, pl.ds(mult(to_x * 128, 128), 128)],
            dxs_ref.at[x, :, pl.ds(mult(n * 256, 256), 256)],
            da_s.at[n, i], da_r.at[n, i], at(x=to_x),
        )

    def dl_copy(n):
        return pltpu.make_async_copy(
            dxown.at[n, pl.ds(mult(x * 128, 128), 128)],
            dxs_ref.at[x, :, pl.ds(mult(n * 256, 256), 256)],
            dl_s.at[n],
        )

    def d_other(n, carry):
        dxsend[n] = ddot(1 - zh, n).astype(BF)
        dz_copy(n).start()
        return carry

    def d_own(n, carry):
        part = ddot(zh, n)
        dz_copy(n).wait_recv()
        dxown[n] = (part + dxrecv[n].astype(F32)).astype(BF)
        for i in range(3):
            da_copy(n, i).start()
        dl_copy(n).start()
        return carry

    wgrad(0)
    c_copies[0].wait_recv()
    wgrad(1)
    c_copies[1].wait_recv()
    for i, half in ((2, 1 - zh), (3, zh)):
        part = cot_copy(i, half * 512, 512)
        copy = remote(part, part, c_s.at[i], c_r.at[i], at(x=hop(x, 2)))
        copy.start()
        c_copies.append(copy)
    wgrad(2)
    stage_a(0)
    for copy in wc_copies:
        copy.wait_recv()
    stage_a(1)
    stage_b(0)
    c_copies[2].wait_recv()
    lax.fori_loop(0, 4, d_other, 0)
    c_copies[3].wait_recv()
    wgrad(3)
    lax.fori_loop(4, 8, d_other, 0)
    stage_b(1)
    stage_a(2)
    lax.fori_loop(0, 4, d_own, 0)
    stage_b(2)
    stage_a(3)
    lax.fori_loop(4, 8, d_own, 0)
    stage_b(3)

    for copy in w_copies + wy_copies + wc_copies + x_copies + xz_copies + c_copies:
        copy.wait_send()
    px_copy(0).wait()
    for r in range(1, 4):
        px_copy(r).wait()

    for r in (2, 3):
        for k in range(4):
            pc_copy(r, k).wait_send()

    def drain_w(r, carry):
        for k in range(3):
            py_copy(r, k).wait_send()
        pz_copy(r).wait_send()
        return carry

    lax.fori_loop(0, 4, drain_w, 0)

    def drain_d(n, carry):
        dz_copy(n).wait_send()
        for i in range(3):
            da_copy(n, i).wait()
        dl_copy(n).wait()
        return carry

    lax.fori_loop(0, 8, drain_d, 0)


def core_call(layer_input, gain, wq, wk, wv, qg, kg, vg, pos, freq):
    vm = pl.BlockSpec(memory_space=pltpu.VMEM)
    hbm = pl.BlockSpec(memory_space=pl.ANY)
    dma = pltpu.SemaphoreType.DMA
    return pl.pallas_call(
        core_kernel,
        out_shape=(
            jax.ShapeDtypeStruct((4, 128, 2048), BF),
            jax.ShapeDtypeStruct((4, 128, 768), BF),
        ),
        in_specs=[vm, vm, hbm, hbm, hbm, vm, vm, vm, vm, vm],
        out_specs=(hbm, hbm),
        scratch_shapes=[
            pltpu.VMEM((4, 16, 128, 128), BF),
            pltpu.VMEM((16, 128, 1024), BF),
            pltpu.VMEM((1024, 3072), BF),
            pltpu.VMEM((16, 128, 3072), BF),
            pltpu.VMEM((2, 4, 256, 768), BF),
            pltpu.VMEM((4, 4, 256, 768), BF),
            pltpu.VMEM((4, 4, 256, 768), BF),
            pltpu.VMEM((4, 3, 256, 768), BF),
            pltpu.VMEM((4, 128, 768), BF),
            pltpu.VMEM((4, 128, 768), BF),
            pltpu.VMEM((4, 128, 768), BF),
            pltpu.VMEM((8, 512, 256), BF),
            pltpu.VMEM((8, 512, 256), BF),
            pltpu.VMEM((8, 512, 256), BF),
            dma((3, 3)), dma((3, 3)), dma((3,)),
            dma((3,)), dma((3,)), dma((4,)), dma((4,)),
            dma((3,)), dma((3,)), dma, dma((4,)), dma((4,)),
            dma((4,)), dma((4,)),
            dma((4, 4)), dma((4, 4)), dma((4, 3)), dma((4, 3)), dma((4,)), dma((4,)),
            dma((3,)), dma((3,)), dma,
            dma((8,)), dma((8,)), dma((8, 3)), dma((8, 3)), dma((8,)),
        ],
        compiler_params=pltpu.CompilerParams(
            collective_id=1, has_side_effects=True, vmem_limit_bytes=63 * 2**20
        ),
        cost_estimate=pl.CostEstimate(flops=26 * 10**9, bytes_accessed=20 * 10**6, transcendentals=0),
        name="projection_backward",
    )(layer_input, gain, wq, wk, wv, qg, kg, vg, pos, freq)


def norm_back_kernel(x_ref, gain_ref, d_ref, o_ref):
    rows = x_ref.shape[0]
    order = [(s, kappa) for s in range(4) for kappa in range(16)]

    def low(s, kappa):
        c, yy, zz = kappa // 8, (kappa // 2) % 4, kappa % 2
        return (yy * 4 + zz * 2 + c) * 512 + s * 128

    square = jnp.zeros((rows, 128), F32)
    cross = jnp.zeros((rows, 128), F32)
    for s, kappa in order:
        cols = pl.ds(low(s, kappa), 128)
        v = x_ref[:, cols].astype(F32)
        g = d_ref[s, :, pl.ds(kappa * 128, 128)].astype(F32) * gain_ref[:, cols]
        square = square + v * v
        cross = cross + v * g
    mean = jnp.sum(square, axis=1, keepdims=True) * (1.0 / 8192)
    rstd = lax.rsqrt(mean + 1e-05)
    dot = jnp.sum(cross, axis=1, keepdims=True) * (1.0 / 8192) * rstd
    for s, kappa in order:
        cols = pl.ds(low(s, kappa), 128)
        v = x_ref[:, cols].astype(F32)
        g = d_ref[s, :, pl.ds(kappa * 128, 128)].astype(F32) * gain_ref[:, cols]
        o_ref[:, cols] = (rstd * (g - (v * rstd) * dot)).astype(BF)


def norm_back(layer_input, gain, parts):
    rows = 32
    return pl.pallas_call(
        norm_back_kernel,
        out_shape=jax.ShapeDtypeStruct((128, 8192), BF),
        grid=(128 // rows,),
        in_specs=[
            pl.BlockSpec((rows, 8192), lambda i: (i, 0)),
            pl.BlockSpec((1, 8192), lambda i: (0, 0)),
            pl.BlockSpec((4, rows, 2048), lambda i: (0, i, 0)),
        ],
        out_specs=pl.BlockSpec((rows, 8192), lambda i: (i, 0)),
        compiler_params=pltpu.CompilerParams(vmem_limit_bytes=32 * 2**20),
        name="norm_backward",
    )(layer_input, gain, parts)


def shards(layer_input, norm_gain, wq, wk, wv, qg, kg, vg, positions):
    gain = norm_gain.reshape(1, 8192)
    index = (jnp.arange(HD, dtype=jnp.int32) % (HD // 2)).astype(F32)
    freq = jnp.exp(-(2.0 * index / HD) * jnp.log(10000.0)).reshape(1, HD)
    parts, sums = core_call(
        layer_input,
        gain,
        wq.reshape(4, 2, 2, 4, 128, 512),
        wk.reshape(4, 2, 2, 4, 128, 128),
        wv.reshape(4, 2, 2, 4, 128, 128),
        qg, kg, vg,
        positions.reshape(8, 128),
        freq,
    )
    input_grad = norm_back(layer_input, gain, parts)
    sums = sums.reshape(512, 768).astype(F32) * (1.0 / math.sqrt(16384))
    return input_grad, sums[:, 512:640], sums[:, 640:], sums[:, :512]


def solution(mesh):
    in_specs = (
        P(("dp", "mp"), None),
        P(),
        P(None, "mp"),
        P(None, "mp"),
        P(None, "mp"),
        P("dp", "mp"),
        P("dp", "mp"),
        P("dp", "mp"),
        P("dp"),
    )
    out_specs = (P(("dp", "mp"), None), P("dp", "mp"), P("dp", "mp"), P("dp", "mp"))
    return jax.shard_map(shards, mesh=mesh, in_specs=in_specs, out_specs=out_specs, check_vma=False)
```

```python
import functools
import math

import jax
import jax.numpy as jnp
import numpy as np
from jax import lax
from jax.experimental import pallas as pl
from jax.experimental.pallas import tpu as pltpu
from jax.sharding import PartitionSpec as P

HD = 128
NY, NX = 4, 4
HOPS = (1, 3, 2)
BF = jnp.bfloat16
F32 = jnp.float32
MESH = pl.DeviceIdType.MESH
FREQ = np.tile(10000.0 ** (-2.0 * np.arange(HD // 2) / HD), 2).astype(np.float32).reshape(1, HD)


def mult(value, by):
    return pl.multiple_of(value, by)


def core_kernel(
    x_ref, gain_ref, wq_ref, wk_ref, wv_ref, q_ref, k_ref, v_ref, pos_ref, freq_ref,
    dxs_ref, dws_ref,
    nt, xst, cot, wb, coresend, sum2, yrel, yrecv, zlsend, zlrecv, xsend, dxsend, dxrecv, dxown,
    w_s, w_r, wl_s, wy_s, wy_r, wq_s, wq_r, wc_s, wc_r, x_s, x_r, xl_s, xz_s, xz_r, c_s, c_r, cq_s, cq_r,
    pc_s, pc_r, ph_s, ph_r, py_s, py_r, pz_s, pz_r, px_s, px_r, pl_s, dz_s, dz_r, da_s, da_r, dl_s,
):
    dp = lax.axis_index("dp")
    mp = lax.axis_index("mp")
    y, zl, core = dp // 4, (dp // 2) % 2, dp % 2
    x, zh = mp // 2, mp % 2

    def at(y=y, zl=zl, core=core, x=x, zh=zh):
        return (y * 4 + zl * 2 + core, x * 2 + zh)

    def hop(v, k):
        return lax.rem(v + k, 4)

    def remote(src, dst, ssem, rsem, where):
        return pltpu.make_async_remote_copy(
            src_ref=src, dst_ref=dst, send_sem=ssem, recv_sem=rsem,
            device_id=where, device_id_type=MESH,
        )

    peers = [at(x=hop(x, k)) for k in HOPS] + [at(y=hop(y, k)) for k in (1, 3)]
    peers += [at(zl=1 - zl), at(zh=1 - zh), at(core=1 - core)]
    barrier = pltpu.get_barrier_semaphore()
    for peer in peers:
        pl.semaphore_signal(barrier, inc=1, device_id=peer, device_id_type=MESH)
    pl.semaphore_wait(barrier, len(peers))

    blocks = (x, hop(x, 3), hop(x, 1), hop(x, 2))
    own_rows = core * 8 + y * 2
    widths = ((wq_ref, 0, 512), (wk_ref, 512, 128), (wv_ref, 640, 128))

    def w_part(j, to_x):
        ref, low, width = widths[j]
        src = ref.at[y, :, core, to_x]
        dst = wb.at[pl.ds(own_rows, 2), :, pl.ds(mult(x * 768 + low, 128), width)]
        return src, dst

    def w_copy(i, j):
        to_x = hop(x, HOPS[i])
        src, dst = w_part(j, to_x)
        return remote(src, dst, w_s.at[i, j], w_r.at[i, j], at(x=to_x))

    def w_start(i):
        for j in range(3):
            w_copy(i, j).start()

    def w_wait(i):
        for j in range(3):
            w_copy(i, j).wait_recv()

    def w_rows(from_y, r):
        rows = pl.ds(core * 8 + from_y * 2, 2)
        if r is None:
            return wb.at[rows]
        return wb.at[rows, :, pl.ds(mult(blocks[r] * 768, 128), 768)]

    def wy_copy(r, s):
        part = w_rows(y, r)
        return remote(part, part, wy_s.at[r, s], wy_r.at[r, s], at(y=hop(y, (1, 3)[s])))

    def wq_copy(r):
        s = r // 2
        part = w_rows(hop(y, (3, 1)[s]), r)
        return remote(part, part, wq_s.at[r], wq_r.at[r], at(y=hop(y, (1, 3)[s])))

    def wc_copy(k):
        part = w_rows(hop(y, k), None)
        return remote(part, part, wc_s.at[k], wc_r.at[k], at(core=1 - core))

    def wy_start(r):
        wy_copy(r, 0).start()
        wy_copy(r, 1).start()

    w_local = []
    for j in range(3):
        src, dst = w_part(j, x)
        copy = pltpu.make_async_copy(src, dst, wl_s.at[j])
        copy.start()
        w_local.append(copy)
    w_start(0)
    w_start(1)
    for copy in w_local:
        copy.wait()
    wy_start(0)

    def squares(c, total):
        piece = x_ref[:, pl.ds(mult(c * 512, 512), 512)].astype(F32)
        piece = piece * piece
        return total + (piece[:, :128] + piece[:, 128:256]) + (piece[:, 256:384] + piece[:, 384:])

    total = lax.fori_loop(0, 16, squares, jnp.zeros((128, 128), F32))
    mean = jnp.sum(total, axis=1, keepdims=True) * (1.0 / 8192)
    rstd = lax.rsqrt(mean + 1e-05)

    def x_to(to_x):
        def block(kappa, carry):
            c, yy, zz = kappa // 8, (kappa // 2) % 4, kappa % 2
            low = mult((yy * 4 + zz * 2 + c) * 512 + to_x * 128, 128)
            rows = x_ref[:, pl.ds(low, 128)].astype(F32)
            normed = rows * rstd * gain_ref[:, pl.ds(low, 128)]
            nt[to_x, kappa] = normed.T.astype(BF)
            return carry

        lax.fori_loop(0, 16, block, 0)

    def x_slot(from_x):
        return xst.at[:, :, pl.ds(mult((zh * 4 + from_x) * 128, 128), 128)]

    def x_copy(i):
        to_x = hop(x, HOPS[i])
        return remote(nt.at[to_x], x_slot(x), x_s.at[i], x_r.at[i], at(x=to_x))

    def xz_copy(i):
        from_x = x if i == 3 else hop(x, 4 - HOPS[i])
        slot = x_slot(from_x)
        return remote(nt.at[x] if i == 3 else slot, slot, xz_s.at[i], xz_r.at[i], at(zh=1 - zh))

    x_to(x)
    x_local = pltpu.make_async_copy(nt.at[x], x_slot(x), xl_s)
    x_local.start()
    xz_copy(3).start()
    for i in (2, 0, 1):
        x_to(hop(x, HOPS[i]))
        x_copy(i).start()
    w_start(2)
    w_wait(0)
    wy_start(1)
    w_wait(1)
    wy_start(2)

    lane = lax.broadcasted_iota(jnp.int32, (128, 128), 1)

    def rope(t, carry):
        block = (t % 4) * 2 + t // 4
        rows = pl.ds(mult(block * 128, 128), 128)
        place = jnp.broadcast_to(pos_ref[pl.ds(block, 1), :].astype(F32), (128, 128)).T
        angle = place * freq_ref[...]
        cosine = jnp.cos(angle)
        sine = jnp.sin(angle)
        sine = jnp.where(lane < 64, sine, -sine)
        out = pl.ds(mult(t * 128, 128), 128)
        for h in range(5):
            v = q_ref[rows, pl.ds(h * 128, 128)] if h < 4 else k_ref[rows, :]
            v = v.astype(F32)
            back = v * cosine + pltpu.roll(v, 64, 1) * sine
            cot[out, pl.ds(mult(x * 768 + h * 128, 128), 128)] = back.astype(BF)
        cot[out, pl.ds(mult(x * 768 + 640, 128), 128)] = v_ref[rows, :]
        return carry

    lax.fori_loop(0, 8, rope, 0)

    def low_row(h):
        return (1 - zh if h == 0 else zh) * 512

    def c_copy(h, s):
        part = cot.at[pl.ds(mult(low_row(h), 512), 512), pl.ds(mult(x * 768, 128), 768)]
        return remote(part, part, c_s.at[h, s], c_r.at[h, s], at(x=hop(x, (1, 3)[s])))

    def cq_copy(h, s):
        b = blocks[1 + s]
        part = cot.at[pl.ds(mult(low_row(h) + s * 256, 256), 256), pl.ds(mult(b * 768, 128), 768)]
        return remote(part, part, cq_s.at[h, s], cq_r.at[h, s], at(x=hop(x, (1, 3)[s])))

    wy_copy(0, 0).wait_recv()
    wq_copy(0).start()
    for i in (0, 1):
        x_copy(i).wait_recv()
        xz_copy(i).start()
    c_copy(0, 0).start()
    c_copy(0, 1).start()
    wy_copy(1, 0).wait_recv()
    wq_copy(1).start()
    wy_copy(2, 1).wait_recv()
    wq_copy(2).start()
    x_copy(2).wait_recv()
    xz_copy(2).start()
    w_wait(2)
    wy_start(3)
    for s in (0, 1):
        c_copy(0, s).wait_recv()
        cq_copy(0, s).start()
    c_copy(1, 0).start()
    c_copy(1, 1).start()
    wy_copy(3, 1).wait_recv()
    wq_copy(3).start()
    wc_copy(0).start()
    for r in (0, 1, 2):
        wy_copy(r, 1 if r < 2 else 0).wait_recv()
    wy_copy(3, 0).wait_recv()
    wc_copy(3).start()
    wc_copy(1).start()
    for r in range(4):
        wq_copy(r).wait_recv()
    wc_copy(2).start()

    def wdot(kappa, b):
        return jnp.dot(
            xst[pl.ds(kappa, 2)].reshape(256, 1024),
            cot[:, pl.ds(mult(b * 768, 128), 768)],
            preferred_element_type=F32,
        )

    def chunk_y(k):
        return hop(y, 6 - k)

    def pc_copy(r, k):
        return remote(coresend.at[r % 2, k], sum2.at[r, k], pc_s.at[r, k], pc_r.at[r, k], at(core=1 - core))

    def ph_copy(r, s):
        src = sum2.at[r, 0, pl.ds(s * 128, 128)]
        return remote(src, yrel.at[r, s], ph_s.at[r, s], ph_r.at[r, s], at(y=hop(y, (1, 3)[s])))

    def py_copy(r, s):
        src = sum2.at[r, (1, 3)[s]]
        return remote(src, yrecv.at[r, s], py_s.at[r, s], py_r.at[r, s], at(y=hop(y, (1, 3)[s])))

    def pz_copy(r):
        return remote(zlsend.at[r], zlrecv.at[r], pz_s.at[r], pz_r.at[r], at(zl=1 - zl))

    def px_copy(r):
        if r == 0:
            return pltpu.make_async_copy(xsend.at[r], dws_ref.at[x], pl_s)
        return remote(xsend.at[r], dws_ref.at[x], px_s.at[r - 1], px_r.at[r - 1], at(x=blocks[r]))

    def wgrad(r):
        b = blocks[r]

        def other(k, carry):
            if r >= 2:
                pc_copy(r - 2, k).wait_send()
            coresend[r % 2, k] = wdot((1 - core) * 8 + chunk_y(k) * 2, b).astype(BF)
            pc_copy(r, k).start()
            return carry

        lax.fori_loop(0, 4, other, 0)

        def own(k, carry):
            part = wdot(core * 8 + chunk_y(k) * 2, b)
            pc_copy(r, k).wait_recv()
            sum2[r, k] = (part + sum2[r, k].astype(F32)).astype(BF)

            @pl.when(k == 0)
            def _():
                ph_copy(r, 0).start()
                ph_copy(r, 1).start()

            return carry

        lax.fori_loop(0, 4, own, 0)

    def wpass(r):
        for s in (0, 1):
            k = (1, 3)[s]
            rows = pl.ds(s * 128, 128)
            ph_copy(r, s).wait_recv()
            sum2[r, k, rows, :] = (sum2[r, k, rows, :].astype(F32) + yrel[r, s].astype(F32)).astype(BF)
            py_copy(r, s).start()

    def y_total(r, low):
        rows = pl.ds(mult(low * 128, 128), 128)
        return sum2[r, 2, rows, :].astype(F32) + (
            yrecv[r, 0, rows, :].astype(F32) + yrecv[r, 1, rows, :].astype(F32)
        )

    def stage_a(r):
        for s in (0, 1):
            py_copy(r, s).wait_recv()
        zlsend[r] = y_total(r, 1 - zl).astype(BF)
        pz_copy(r).start()

    def stage_b(r):
        pz_copy(r).wait_recv()
        xsend[r] = (y_total(r, zl) + zlrecv[r].astype(F32)).astype(BF)
        px_copy(r).start()

    def ddot(half, n):
        return lax.dot_general(
            cot[pl.ds(mult(half * 512, 512), 512), :],
            wb[pl.ds(n * 2, 2)].reshape(256, 3072),
            (((1,), (1,)), ((), ())),
            preferred_element_type=F32,
        )

    def dz_copy(n):
        return remote(dxsend.at[n], dxrecv.at[n], dz_s.at[n], dz_r.at[n], at(zh=1 - zh))

    def da_copy(n, i):
        to_x = hop(x, HOPS[i])
        return remote(
            dxown.at[n, pl.ds(mult(to_x * 128, 128), 128)],
            dxs_ref.at[x, :, pl.ds(mult(n * 256, 256), 256)],
            da_s.at[n, i], da_r.at[n, i], at(x=to_x),
        )

    def dl_copy(n):
        return pltpu.make_async_copy(
            dxown.at[n, pl.ds(mult(x * 128, 128), 128)],
            dxs_ref.at[x, :, pl.ds(mult(n * 256, 256), 256)],
            dl_s.at[n],
        )

    def d_other(n, carry):
        dxsend[n] = ddot(1 - zh, n).astype(BF)
        dz_copy(n).start()
        return carry

    def d_own(n, carry):
        part = ddot(zh, n)
        dz_copy(n).wait_recv()
        dxown[n] = (part + dxrecv[n].astype(F32)).astype(BF)
        for i in (2, 0, 1):
            da_copy(n, i).start()
        dl_copy(n).start()
        return carry

    x_local.wait()
    for i in (3, 0, 1, 2):
        xz_copy(i).wait_recv()
    wgrad(0)
    for s in (0, 1):
        cq_copy(0, s).wait_recv()
    for k in range(4):
        wc_copy(k).wait_recv()
    lax.fori_loop(0, 4, d_other, 0)
    wpass(0)
    lax.fori_loop(4, 8, d_other, 0)
    for s in (0, 1):
        c_copy(1, s).wait_recv()
        cq_copy(1, s).start()
    wgrad(1)
    wgrad(2)
    wpass(1)
    stage_a(0)
    for s in (0, 1):
        cq_copy(1, s).wait_recv()
    wpass(2)
    wgrad(3)
    stage_b(0)
    wpass(3)
    lax.fori_loop(0, 3, d_own, 0)
    stage_a(1)
    lax.fori_loop(3, 5, d_own, 0)
    stage_b(1)
    stage_a(2)
    lax.fori_loop(5, 7, d_own, 0)
    stage_b(2)
    stage_a(3)
    lax.fori_loop(7, 8, d_own, 0)
    stage_b(3)

    for i in range(3):
        for j in range(3):
            w_copy(i, j).wait_send()
        x_copy(i).wait_send()
    for r in range(4):
        wy_copy(r, 0).wait_send()
        wy_copy(r, 1).wait_send()
        wq_copy(r).wait_send()
        wc_copy(r).wait_send()
        xz_copy(r).wait_send()
    for h in (0, 1):
        for s in (0, 1):
            c_copy(h, s).wait_send()
            cq_copy(h, s).wait_send()
    for r in (2, 3):
        for k in range(4):
            pc_copy(r, k).wait_send()
    for r in range(4):
        for s in (0, 1):
            ph_copy(r, s).wait_send()
            py_copy(r, s).wait_send()
        pz_copy(r).wait_send()
        px_copy(r).wait()

    def drain(n, carry):
        dz_copy(n).wait_send()
        for i in range(3):
            da_copy(n, i).wait()
        dl_copy(n).wait()
        return carry

    lax.fori_loop(0, 8, drain, 0)


def core_call(layer_input, gain, wq, wk, wv, qg, kg, vg, pos, freq):
    vm = pl.BlockSpec(memory_space=pltpu.VMEM)
    hbm = pl.BlockSpec(memory_space=pl.ANY)
    dma = pltpu.SemaphoreType.DMA
    return pl.pallas_call(
        core_kernel,
        out_shape=(
            jax.ShapeDtypeStruct((4, 128, 2048), BF),
            jax.ShapeDtypeStruct((4, 128, 768), BF),
        ),
        in_specs=[vm, vm, hbm, hbm, hbm, vm, vm, vm, vm, vm],
        out_specs=(hbm, hbm),
        scratch_shapes=[
            pltpu.VMEM((4, 16, 128, 128), BF),
            pltpu.VMEM((16, 128, 1024), BF),
            pltpu.VMEM((1024, 3072), BF),
            pltpu.VMEM((16, 128, 3072), BF),
            pltpu.VMEM((2, 4, 256, 768), BF),
            pltpu.VMEM((4, 4, 256, 768), BF),
            pltpu.VMEM((4, 2, 128, 768), BF),
            pltpu.VMEM((4, 2, 256, 768), BF),
            pltpu.VMEM((4, 128, 768), BF),
            pltpu.VMEM((4, 128, 768), BF),
            pltpu.VMEM((4, 128, 768), BF),
            pltpu.VMEM((8, 512, 256), BF),
            pltpu.VMEM((8, 512, 256), BF),
            pltpu.VMEM((8, 512, 256), BF),
            dma((3, 3)), dma((3, 3)), dma((3,)),
            dma((4, 2)), dma((4, 2)), dma((4,)), dma((4,)), dma((4,)), dma((4,)),
            dma((3,)), dma((3,)), dma, dma((4,)), dma((4,)),
            dma((2, 2)), dma((2, 2)), dma((2, 2)), dma((2, 2)),
            dma((4, 4)), dma((4, 4)), dma((4, 2)), dma((4, 2)), dma((4, 2)), dma((4, 2)), dma((4,)), dma((4,)),
            dma((3,)), dma((3,)), dma,
            dma((8,)), dma((8,)), dma((8, 3)), dma((8, 3)), dma((8,)),
        ],
        compiler_params=pltpu.CompilerParams(
            collective_id=1, has_side_effects=True, vmem_limit_bytes=63 * 2**20
        ),
        cost_estimate=pl.CostEstimate(flops=26 * 10**9, bytes_accessed=20 * 10**6, transcendentals=0),
        name="projection_backward",
    )(layer_input, gain, wq, wk, wv, qg, kg, vg, pos, freq)


def norm_back_kernel(x_ref, gain_ref, d_ref, s_ref, o_ref, k_ref, v_ref, q_ref):
    rows = x_ref.shape[0]
    order = [(s, kappa) for s in range(4) for kappa in range(16)]
    factor = 1.0 / math.sqrt(16384)
    q_ref[...] = s_ref[0, :, :512].astype(F32) * factor
    k_ref[...] = s_ref[0, :, 512:640].astype(F32) * factor
    v_ref[...] = s_ref[0, :, 640:].astype(F32) * factor

    def low(s, kappa):
        c, yy, zz = kappa // 8, (kappa // 2) % 4, kappa % 2
        return (yy * 4 + zz * 2 + c) * 512 + s * 128

    square = jnp.zeros((rows, 128), F32)
    cross = jnp.zeros((rows, 128), F32)
    for s, kappa in order:
        cols = pl.ds(low(s, kappa), 128)
        v = x_ref[:, cols].astype(F32)
        g = d_ref[s, :, pl.ds(kappa * 128, 128)].astype(F32) * gain_ref[:, cols]
        square = square + v * v
        cross = cross + v * g
    mean = jnp.sum(square, axis=1, keepdims=True) * (1.0 / 8192)
    rstd = lax.rsqrt(mean + 1e-05)
    dot = jnp.sum(cross, axis=1, keepdims=True) * (1.0 / 8192) * rstd
    for s, kappa in order:
        cols = pl.ds(low(s, kappa), 128)
        v = x_ref[:, cols].astype(F32)
        g = d_ref[s, :, pl.ds(kappa * 128, 128)].astype(F32) * gain_ref[:, cols]
        o_ref[:, cols] = (rstd * (g - (v * rstd) * dot)).astype(BF)


def norm_back(layer_input, gain, parts, sums):
    rows = 32

    def out(width):
        return pl.BlockSpec((128, width), lambda i: (i, 0))

    return pl.pallas_call(
        norm_back_kernel,
        out_shape=(
            jax.ShapeDtypeStruct((128, 8192), BF),
            jax.ShapeDtypeStruct((512, 128), F32),
            jax.ShapeDtypeStruct((512, 128), F32),
            jax.ShapeDtypeStruct((512, 512), F32),
        ),
        grid=(128 // rows,),
        in_specs=[
            pl.BlockSpec((rows, 8192), lambda i: (i, 0)),
            pl.BlockSpec((1, 8192), lambda i: (0, 0)),
            pl.BlockSpec((4, rows, 2048), lambda i: (0, i, 0)),
            pl.BlockSpec((1, 128, 768), lambda i: (i, 0, 0)),
        ],
        out_specs=(pl.BlockSpec((rows, 8192), lambda i: (i, 0)), out(128), out(128), out(512)),
        compiler_params=pltpu.CompilerParams(vmem_limit_bytes=63 * 2**20),
        name="norm_backward",
    )(layer_input, gain, parts, sums)


def shards(layer_input, norm_gain, wq, wk, wv, qg, kg, vg, positions):
    gain = norm_gain.reshape(1, 8192)
    parts, sums = core_call(
        layer_input,
        gain,
        wq.reshape(4, 2, 2, 4, 128, 512),
        wk.reshape(4, 2, 2, 4, 128, 128),
        wv.reshape(4, 2, 2, 4, 128, 128),
        qg, kg, vg,
        positions.reshape(8, 128),
        jnp.asarray(FREQ),
    )
    return norm_back(layer_input, gain, parts, sums)


def solution(mesh):
    in_specs = (
        P(("dp", "mp"), None),
        P(),
        P(None, "mp"),
        P(None, "mp"),
        P(None, "mp"),
        P("dp", "mp"),
        P("dp", "mp"),
        P("dp", "mp"),
        P("dp"),
    )
    out_specs = (P(("dp", "mp"), None), P("dp", "mp"), P("dp", "mp"), P("dp", "mp"))
    return jax.shard_map(shards, mesh=mesh, in_specs=in_specs, out_specs=out_specs, check_vma=False)
```

```python
import functools
import math

import jax
import jax.numpy as jnp
import numpy as np
from jax import lax
from jax.experimental import pallas as pl
from jax.experimental.pallas import tpu as pltpu
from jax.sharding import PartitionSpec as P

HD = 128
NY, NX = 4, 4
HOPS = (1, 3, 2)
BF = jnp.bfloat16
F32 = jnp.float32
MESH = pl.DeviceIdType.MESH
FREQ = np.tile(10000.0 ** (-2.0 * np.arange(HD // 2) / HD), 2).astype(np.float32).reshape(1, HD)


def mult(value, by):
    return pl.multiple_of(value, by)


def core_kernel(
    x_ref, gain_ref, wq_ref, wk_ref, wv_ref, q_ref, k_ref, v_ref, pos_ref, freq_ref,
    dxs_ref, dws_ref,
    nt, xst, cot, wb, coresend, sum2, yrel, yrecv, zlsend, zlrecv, xsend, dxsend, dxrecv, dxown,
    w_s, w_r, wl_s, wz_s, wz_r, wy_s, wy_r, wq_s, wq_r, wc_s, wc_r, x_s, x_r, xl_s, xz_s, xz_r, c_s, c_r, cq_s, cq_r,
    pc_s, pc_r, ph_s, ph_r, py_s, py_r, pz_s, pz_r, px_s, px_r, pl_s, dz_s, dz_r, da_s, da_r, dl_s,
):
    dp = lax.axis_index("dp")
    mp = lax.axis_index("mp")
    y, zl, core = dp // 4, (dp // 2) % 2, dp % 2
    x, zh = mp // 2, mp % 2

    def at(y=y, zl=zl, core=core, x=x, zh=zh):
        return (y * 4 + zl * 2 + core, x * 2 + zh)

    def hop(v, k):
        return lax.rem(v + k, 4)

    def remote(src, dst, ssem, rsem, where):
        return pltpu.make_async_remote_copy(
            src_ref=src, dst_ref=dst, send_sem=ssem, recv_sem=rsem,
            device_id=where, device_id_type=MESH,
        )

    peers = [at(x=hop(x, k)) for k in HOPS] + [at(y=hop(y, k)) for k in (1, 3)]
    peers += [at(zl=1 - zl), at(zh=1 - zh), at(core=1 - core)]
    barrier = pltpu.get_barrier_semaphore()
    for peer in peers:
        pl.semaphore_signal(barrier, inc=1, device_id=peer, device_id_type=MESH)
    pl.semaphore_wait(barrier, len(peers))

    blocks = (x, hop(x, 3), hop(x, 1), hop(x, 2))
    own_rows = core * 8 + y * 2
    widths = ((wq_ref, 0, 512), (wk_ref, 512, 128), (wv_ref, 640, 128))

    def w_copy(i, j):
        ref, low, width = widths[j]
        to_x = hop(x, HOPS[i])
        dst = wb.at[own_rows + zl, :, pl.ds(mult(x * 768 + low, 128), width)]
        return remote(ref.at[y, zl, core, to_x], dst, w_s.at[i, j], w_r.at[i, j], at(x=to_x))

    def wz_copy(r):
        part = wb.at[own_rows + zl, :, pl.ds(mult(blocks[r] * 768, 128), 768)]
        return remote(part, part, wz_s.at[r], wz_r.at[r], at(zl=1 - zl))

    def w_start(i):
        for j in range(3):
            w_copy(i, j).start()

    def w_wait(i):
        for j in range(3):
            w_copy(i, j).wait_recv()

    def w_rows(from_y, r):
        rows = pl.ds(core * 8 + from_y * 2, 2)
        if r is None:
            return wb.at[rows]
        return wb.at[rows, :, pl.ds(mult(blocks[r] * 768, 128), 768)]

    def wy_copy(r, s):
        part = w_rows(y, r)
        return remote(part, part, wy_s.at[r, s], wy_r.at[r, s], at(y=hop(y, (1, 3)[s])))

    def wq_copy(r):
        s = r // 2
        part = w_rows(hop(y, (3, 1)[s]), r)
        return remote(part, part, wq_s.at[r], wq_r.at[r], at(y=hop(y, (1, 3)[s])))

    def wc_copy(k):
        part = w_rows(hop(y, k), None)
        return remote(part, part, wc_s.at[k], wc_r.at[k], at(core=1 - core))

    def wy_start(r):
        wy_copy(r, 0).start()
        wy_copy(r, 1).start()

    w_local = []
    for j in range(3):
        ref, low, width = widths[j]
        src = ref.at[y, :, core, x]
        dst = wb.at[pl.ds(own_rows, 2), :, pl.ds(mult(x * 768 + low, 128), width)]
        copy = pltpu.make_async_copy(src, dst, wl_s.at[j])
        copy.start()
        w_local.append(copy)
    w_start(0)
    w_start(1)
    w_start(2)
    for copy in w_local:
        copy.wait()
    wy_start(0)

    def squares(c, total):
        piece = x_ref[:, pl.ds(mult(c * 512, 512), 512)].astype(F32)
        piece = piece * piece
        return total + (piece[:, :128] + piece[:, 128:256]) + (piece[:, 256:384] + piece[:, 384:])

    total = lax.fori_loop(0, 16, squares, jnp.zeros((128, 128), F32))
    mean = jnp.sum(total, axis=1, keepdims=True) * (1.0 / 8192)
    rstd = lax.rsqrt(mean + 1e-05)

    def x_to(to_x):
        def block(kappa, carry):
            c, yy, zz = kappa // 8, (kappa // 2) % 4, kappa % 2
            low = mult((yy * 4 + zz * 2 + c) * 512 + to_x * 128, 128)
            rows = x_ref[:, pl.ds(low, 128)].astype(F32)
            normed = rows * rstd * gain_ref[:, pl.ds(low, 128)]
            nt[to_x, kappa] = normed.T.astype(BF)
            return carry

        lax.fori_loop(0, 16, block, 0)

    def x_slot(from_x):
        return xst.at[:, :, pl.ds(mult((zh * 4 + from_x) * 128, 128), 128)]

    def x_copy(i):
        to_x = hop(x, HOPS[i])
        return remote(nt.at[to_x], x_slot(x), x_s.at[i], x_r.at[i], at(x=to_x))

    def xz_copy(i):
        from_x = x if i == 3 else hop(x, 4 - HOPS[i])
        slot = x_slot(from_x)
        return remote(nt.at[x] if i == 3 else slot, slot, xz_s.at[i], xz_r.at[i], at(zh=1 - zh))

    x_to(x)
    x_local = pltpu.make_async_copy(nt.at[x], x_slot(x), xl_s)
    x_local.start()
    xz_copy(3).start()
    for i in range(3):
        x_to(hop(x, HOPS[i]))
        x_copy(i).start()
    for i in range(3):
        w_wait(i)
        wz_copy(i + 1).start()
    for r in (1, 2):
        wz_copy(r).wait_recv()
        wy_start(r)

    lane = lax.broadcasted_iota(jnp.int32, (128, 128), 1)

    def rope(t, carry):
        block = (t % 4) * 2 + t // 4
        rows = pl.ds(mult(block * 128, 128), 128)
        place = jnp.broadcast_to(pos_ref[pl.ds(block, 1), :].astype(F32), (128, 128)).T
        angle = place * freq_ref[...]
        cosine = jnp.cos(angle)
        sine = jnp.sin(angle)
        sine = jnp.where(lane < 64, sine, -sine)
        out = pl.ds(mult(t * 128, 128), 128)
        for h in range(5):
            v = q_ref[rows, pl.ds(h * 128, 128)] if h < 4 else k_ref[rows, :]
            v = v.astype(F32)
            back = v * cosine + pltpu.roll(v, 64, 1) * sine
            cot[out, pl.ds(mult(x * 768 + h * 128, 128), 128)] = back.astype(BF)
        cot[out, pl.ds(mult(x * 768 + 640, 128), 128)] = v_ref[rows, :]
        return carry

    lax.fori_loop(0, 8, rope, 0)

    def low_row(h):
        return (1 - zh if h == 0 else zh) * 512

    def c_copy(h, s):
        part = cot.at[pl.ds(mult(low_row(h), 512), 512), pl.ds(mult(x * 768, 128), 768)]
        return remote(part, part, c_s.at[h, s], c_r.at[h, s], at(x=hop(x, (1, 3)[s])))

    def cq_copy(h, s):
        b = blocks[1 + s]
        part = cot.at[pl.ds(mult(low_row(h) + s * 256, 256), 256), pl.ds(mult(b * 768, 128), 768)]
        return remote(part, part, cq_s.at[h, s], cq_r.at[h, s], at(x=hop(x, (1, 3)[s])))

    wy_copy(0, 0).wait_recv()
    wq_copy(0).start()
    for i in (0, 1):
        x_copy(i).wait_recv()
        xz_copy(i).start()
    wz_copy(3).wait_recv()
    wy_start(3)
    wy_copy(1, 0).wait_recv()
    wq_copy(1).start()
    wy_copy(2, 1).wait_recv()
    wq_copy(2).start()
    x_copy(2).wait_recv()
    xz_copy(2).start()
    c_copy(0, 0).start()
    c_copy(0, 1).start()
    wc_copy(0).start()
    wy_copy(3, 1).wait_recv()
    wq_copy(3).start()
    for s in (0, 1):
        c_copy(0, s).wait_recv()
        cq_copy(0, s).start()
    for r in (0, 1, 2):
        wy_copy(r, 1 if r < 2 else 0).wait_recv()
    wy_copy(3, 0).wait_recv()
    wc_copy(3).start()
    wc_copy(1).start()
    for r in range(4):
        wq_copy(r).wait_recv()
    wc_copy(2).start()
    for s in (0, 1):
        cq_copy(0, s).wait_send()
        c_copy(1, s).start()

    def wdot(kappa, b):
        return jnp.dot(
            xst[pl.ds(kappa, 2)].reshape(256, 1024),
            cot[:, pl.ds(mult(b * 768, 128), 768)],
            preferred_element_type=F32,
        )

    def chunk_y(k):
        return hop(y, 6 - k)

    def pc_copy(r, k):
        return remote(coresend.at[r % 2, k], sum2.at[r, k], pc_s.at[r, k], pc_r.at[r, k], at(core=1 - core))

    def ph_copy(r, s):
        src = sum2.at[r, 0, pl.ds(s * 128, 128)]
        return remote(src, yrel.at[r, s], ph_s.at[r, s], ph_r.at[r, s], at(y=hop(y, (1, 3)[s])))

    def py_copy(r, s):
        src = sum2.at[r, (1, 3)[s]]
        return remote(src, yrecv.at[r, s], py_s.at[r, s], py_r.at[r, s], at(y=hop(y, (1, 3)[s])))

    def pz_copy(r):
        return remote(zlsend.at[r], zlrecv.at[r], pz_s.at[r], pz_r.at[r], at(zl=1 - zl))

    def px_copy(r):
        if r == 0:
            return pltpu.make_async_copy(xsend.at[r], dws_ref.at[x], pl_s)
        return remote(xsend.at[r], dws_ref.at[x], px_s.at[r - 1], px_r.at[r - 1], at(x=blocks[r]))

    def wother(r):
        b = blocks[r]

        def other(k, carry):
            if r >= 2:
                pc_copy(r - 2, k).wait_send()
            coresend[r % 2, k] = wdot((1 - core) * 8 + chunk_y(k) * 2, b).astype(BF)
            pc_copy(r, k).start()
            return carry

        lax.fori_loop(0, 4, other, 0)

    def wown(r):
        b = blocks[r]

        def own(k, carry):
            part = wdot(core * 8 + chunk_y(k) * 2, b)
            pc_copy(r, k).wait_recv()
            sum2[r, k] = (part + sum2[r, k].astype(F32)).astype(BF)

            @pl.when(k == 0)
            def _():
                ph_copy(r, 0).start()
                ph_copy(r, 1).start()

            return carry

        lax.fori_loop(0, 4, own, 0)

    def wpass(r):
        for s in (0, 1):
            k = (1, 3)[s]
            rows = pl.ds(s * 128, 128)
            ph_copy(r, s).wait_recv()
            sum2[r, k, rows, :] = (sum2[r, k, rows, :].astype(F32) + yrel[r, s].astype(F32)).astype(BF)
            py_copy(r, s).start()

    def y_total(r, low):
        rows = pl.ds(mult(low * 128, 128), 128)
        return sum2[r, 2, rows, :].astype(F32) + (
            yrecv[r, 0, rows, :].astype(F32) + yrecv[r, 1, rows, :].astype(F32)
        )

    def stage_a(r):
        for s in (0, 1):
            py_copy(r, s).wait_recv()
        zlsend[r] = y_total(r, 1 - zl).astype(BF)
        pz_copy(r).start()

    def stage_b(r):
        pz_copy(r).wait_recv()
        xsend[r] = (y_total(r, zl) + zlrecv[r].astype(F32)).astype(BF)
        px_copy(r).start()

    def ddot(half, n):
        return lax.dot_general(
            cot[pl.ds(mult(half * 512, 512), 512), :],
            wb[pl.ds(n * 2, 2)].reshape(256, 3072),
            (((1,), (1,)), ((), ())),
            preferred_element_type=F32,
        )

    def dz_copy(n):
        return remote(dxsend.at[n], dxrecv.at[n], dz_s.at[n], dz_r.at[n], at(zh=1 - zh))

    def da_copy(n, i):
        to_x = hop(x, HOPS[i])
        return remote(
            dxown.at[n, pl.ds(mult(to_x * 128, 128), 128)],
            dxs_ref.at[x, :, pl.ds(mult(n * 256, 256), 256)],
            da_s.at[n, i], da_r.at[n, i], at(x=to_x),
        )

    def dl_copy(n):
        return pltpu.make_async_copy(
            dxown.at[n, pl.ds(mult(x * 128, 128), 128)],
            dxs_ref.at[x, :, pl.ds(mult(n * 256, 256), 256)],
            dl_s.at[n],
        )

    def d_other(n, carry):
        dxsend[n] = ddot(1 - zh, n).astype(BF)
        dz_copy(n).start()
        return carry

    def d_own(n, carry):
        part = ddot(zh, n)
        dz_copy(n).wait_recv()
        dxown[n] = (part + dxrecv[n].astype(F32)).astype(BF)
        for i in (2, 0, 1):
            da_copy(n, i).start()
        dl_copy(n).start()
        return carry

    x_local.wait()
    for i in (3, 0, 1, 2):
        xz_copy(i).wait_recv()
    wother(0)
    wown(0)
    for s in (0, 1):
        cq_copy(0, s).wait_recv()
    for k in range(4):
        wc_copy(k).wait_recv()
    lax.fori_loop(0, 3, d_other, 0)
    wpass(0)
    lax.fori_loop(3, 8, d_other, 0)
    for s in (0, 1):
        c_copy(1, s).wait_recv()
        cq_copy(1, s).start()
    wother(1)
    wown(1)
    wother(2)
    wpass(1)
    wown(2)
    for s in (0, 1):
        cq_copy(1, s).wait_recv()
    wother(3)
    wpass(2)
    wown(3)
    lax.fori_loop(0, 2, d_own, 0)
    wpass(3)
    lax.fori_loop(2, 4, d_own, 0)
    stage_a(0)
    lax.fori_loop(4, 6, d_own, 0)
    stage_a(1)
    stage_b(0)
    stage_a(2)
    lax.fori_loop(6, 7, d_own, 0)
    stage_b(1)
    stage_b(2)
    stage_a(3)
    lax.fori_loop(7, 8, d_own, 0)
    stage_b(3)

    for i in range(3):
        for j in range(3):
            w_copy(i, j).wait_send()
        x_copy(i).wait_send()
    for r in range(4):
        if r > 0:
            wz_copy(r).wait_send()
        wy_copy(r, 0).wait_send()
        wy_copy(r, 1).wait_send()
        wq_copy(r).wait_send()
        wc_copy(r).wait_send()
        xz_copy(r).wait_send()
    for h in (0, 1):
        for s in (0, 1):
            c_copy(h, s).wait_send()
            if h == 1:
                cq_copy(h, s).wait_send()
    for r in (2, 3):
        for k in range(4):
            pc_copy(r, k).wait_send()
    for r in range(4):
        for s in (0, 1):
            ph_copy(r, s).wait_send()
            py_copy(r, s).wait_send()
        pz_copy(r).wait_send()
        px_copy(r).wait()

    def drain(n, carry):
        dz_copy(n).wait_send()
        for i in range(3):
            da_copy(n, i).wait()
        dl_copy(n).wait()
        return carry

    lax.fori_loop(0, 8, drain, 0)


def core_call(layer_input, gain, wq, wk, wv, qg, kg, vg, pos, freq):
    vm = pl.BlockSpec(memory_space=pltpu.VMEM)
    hbm = pl.BlockSpec(memory_space=pl.ANY)
    dma = pltpu.SemaphoreType.DMA
    return pl.pallas_call(
        core_kernel,
        out_shape=(
            jax.ShapeDtypeStruct((4, 128, 2048), BF),
            jax.ShapeDtypeStruct((4, 128, 768), BF),
        ),
        in_specs=[vm, vm, hbm, hbm, hbm, vm, vm, vm, vm, vm],
        out_specs=(hbm, hbm),
        scratch_shapes=[
            pltpu.VMEM((4, 16, 128, 128), BF),
            pltpu.VMEM((16, 128, 1024), BF),
            pltpu.VMEM((1024, 3072), BF),
            pltpu.VMEM((16, 128, 3072), BF),
            pltpu.VMEM((2, 4, 256, 768), BF),
            pltpu.VMEM((4, 4, 256, 768), BF),
            pltpu.VMEM((4, 2, 128, 768), BF),
            pltpu.VMEM((4, 2, 256, 768), BF),
            pltpu.VMEM((4, 128, 768), BF),
            pltpu.VMEM((4, 128, 768), BF),
            pltpu.VMEM((4, 128, 768), BF),
            pltpu.VMEM((8, 512, 256), BF),
            pltpu.VMEM((8, 512, 256), BF),
            pltpu.VMEM((8, 512, 256), BF),
            dma((3, 3)), dma((3, 3)), dma((3,)), dma((4,)), dma((4,)),
            dma((4, 2)), dma((4, 2)), dma((4,)), dma((4,)), dma((4,)), dma((4,)),
            dma((3,)), dma((3,)), dma, dma((4,)), dma((4,)),
            dma((2, 2)), dma((2, 2)), dma((2, 2)), dma((2, 2)),
            dma((4, 4)), dma((4, 4)), dma((4, 2)), dma((4, 2)), dma((4, 2)), dma((4, 2)), dma((4,)), dma((4,)),
            dma((3,)), dma((3,)), dma,
            dma((8,)), dma((8,)), dma((8, 3)), dma((8, 3)), dma((8,)),
        ],
        compiler_params=pltpu.CompilerParams(
            collective_id=1, has_side_effects=True, vmem_limit_bytes=63 * 2**20
        ),
        cost_estimate=pl.CostEstimate(flops=26 * 10**9, bytes_accessed=20 * 10**6, transcendentals=0),
        name="projection_backward",
    )(layer_input, gain, wq, wk, wv, qg, kg, vg, pos, freq)


def norm_back_kernel(x_ref, gain_ref, d_ref, s_ref, o_ref, k_ref, v_ref, q_ref):
    rows = x_ref.shape[0]
    order = [(s, kappa) for s in range(4) for kappa in range(16)]
    factor = 1.0 / math.sqrt(16384)
    q_ref[...] = s_ref[0, :, :512].astype(F32) * factor
    k_ref[...] = s_ref[0, :, 512:640].astype(F32) * factor
    v_ref[...] = s_ref[0, :, 640:].astype(F32) * factor

    def low(s, kappa):
        c, yy, zz = kappa // 8, (kappa // 2) % 4, kappa % 2
        return (yy * 4 + zz * 2 + c) * 512 + s * 128

    square = jnp.zeros((rows, 128), F32)
    cross = jnp.zeros((rows, 128), F32)
    for s, kappa in order:
        cols = pl.ds(low(s, kappa), 128)
        v = x_ref[:, cols].astype(F32)
        g = d_ref[s, :, pl.ds(kappa * 128, 128)].astype(F32) * gain_ref[:, cols]
        square = square + v * v
        cross = cross + v * g
    mean = jnp.sum(square, axis=1, keepdims=True) * (1.0 / 8192)
    rstd = lax.rsqrt(mean + 1e-05)
    dot = jnp.sum(cross, axis=1, keepdims=True) * (1.0 / 8192) * rstd
    for s, kappa in order:
        cols = pl.ds(low(s, kappa), 128)
        v = x_ref[:, cols].astype(F32)
        g = d_ref[s, :, pl.ds(kappa * 128, 128)].astype(F32) * gain_ref[:, cols]
        o_ref[:, cols] = (rstd * (g - (v * rstd) * dot)).astype(BF)


def norm_back(layer_input, gain, parts, sums):
    rows = 32

    def out(width):
        return pl.BlockSpec((128, width), lambda i: (i, 0))

    return pl.pallas_call(
        norm_back_kernel,
        out_shape=(
            jax.ShapeDtypeStruct((128, 8192), BF),
            jax.ShapeDtypeStruct((512, 128), F32),
            jax.ShapeDtypeStruct((512, 128), F32),
            jax.ShapeDtypeStruct((512, 512), F32),
        ),
        grid=(128 // rows,),
        in_specs=[
            pl.BlockSpec((rows, 8192), lambda i: (i, 0)),
            pl.BlockSpec((1, 8192), lambda i: (0, 0)),
            pl.BlockSpec((4, rows, 2048), lambda i: (0, i, 0)),
            pl.BlockSpec((1, 128, 768), lambda i: (i, 0, 0)),
        ],
        out_specs=(pl.BlockSpec((rows, 8192), lambda i: (i, 0)), out(128), out(128), out(512)),
        compiler_params=pltpu.CompilerParams(vmem_limit_bytes=63 * 2**20),
        name="norm_backward",
    )(layer_input, gain, parts, sums)


def shards(layer_input, norm_gain, wq, wk, wv, qg, kg, vg, positions):
    gain = norm_gain.reshape(1, 8192)
    parts, sums = core_call(
        layer_input,
        gain,
        wq.reshape(4, 2, 2, 4, 128, 512),
        wk.reshape(4, 2, 2, 4, 128, 128),
        wv.reshape(4, 2, 2, 4, 128, 128),
        qg, kg, vg,
        positions.reshape(8, 128),
        jnp.asarray(FREQ),
    )
    return norm_back(layer_input, gain, parts, sums)


def solution(mesh):
    in_specs = (
        P(("dp", "mp"), None),
        P(),
        P(None, "mp"),
        P(None, "mp"),
        P(None, "mp"),
        P("dp", "mp"),
        P("dp", "mp"),
        P("dp", "mp"),
        P("dp"),
    )
    out_specs = (P(("dp", "mp"), None), P("dp", "mp"), P("dp", "mp"), P("dp", "mp"))
    return jax.shard_map(shards, mesh=mesh, in_specs=in_specs, out_specs=out_specs, check_vma=False)
```

```python
import functools
import math

import jax
import jax.numpy as jnp
import numpy as np
from jax import lax
from jax.experimental import pallas as pl
from jax.experimental.pallas import tpu as pltpu
from jax.sharding import PartitionSpec as P

HD = 128
NY, NX = 4, 4
HOPS = (1, 3, 2)
BF = jnp.bfloat16
F32 = jnp.float32
MESH = pl.DeviceIdType.MESH
FREQ = np.tile(10000.0 ** (-2.0 * np.arange(HD // 2) / HD), 2).astype(np.float32).reshape(1, HD)


def mult(value, by):
    return pl.multiple_of(value, by)


def core_kernel(
    x_ref, gain_ref, wq_ref, wk_ref, wv_ref, q_ref, k_ref, v_ref, pos_ref, freq_ref,
    dxs_ref, dws_ref,
    nt, xst, cot, wb, coresend, sum2, yrel, yrecv, zlsend, zlrecv, xsend, dxsend, dxrecv, dxown,
    w_s, w_r, wl_s, wz_s, wz_r, wy_s, wy_r, wq_s, wq_r, wc_s, wc_r, x_s, x_r, xl_s, xz_s, xz_r, c_s, c_r, cq_s, cq_r,
    pc_s, pc_r, ph_s, ph_r, py_s, py_r, pz_s, pz_r, px_s, px_r, pl_s, dz_s, dz_r, da_s, da_r, dl_s,
):
    dp = lax.axis_index("dp")
    mp = lax.axis_index("mp")
    y, zl, core = dp // 4, (dp // 2) % 2, dp % 2
    x, zh = mp // 2, mp % 2

    def at(y=y, zl=zl, core=core, x=x, zh=zh):
        return (y * 4 + zl * 2 + core, x * 2 + zh)

    def hop(v, k):
        return lax.rem(v + k, 4)

    def remote(src, dst, ssem, rsem, where):
        return pltpu.make_async_remote_copy(
            src_ref=src, dst_ref=dst, send_sem=ssem, recv_sem=rsem,
            device_id=where, device_id_type=MESH,
        )

    peers = [at(x=hop(x, k)) for k in HOPS] + [at(y=hop(y, k)) for k in (1, 3)]
    peers += [at(zl=1 - zl), at(zh=1 - zh), at(core=1 - core)]
    barrier = pltpu.get_barrier_semaphore()
    for peer in peers:
        pl.semaphore_signal(barrier, inc=1, device_id=peer, device_id_type=MESH)
    pl.semaphore_wait(barrier, len(peers))

    blocks = (x, hop(x, 3), hop(x, 1), hop(x, 2))
    own_rows = core * 8 + y * 2
    widths = ((wq_ref, 0, 512), (wk_ref, 512, 128), (wv_ref, 640, 128))

    def w_copy(i, j):
        ref, low, width = widths[j]
        to_x = hop(x, HOPS[i])
        dst = wb.at[own_rows + zl, :, pl.ds(mult(x * 768 + low, 128), width)]
        return remote(ref.at[y, zl, core, to_x], dst, w_s.at[i, j], w_r.at[i, j], at(x=to_x))

    def wz_copy(r):
        part = wb.at[own_rows + zl, :, pl.ds(mult(blocks[r] * 768, 128), 768)]
        return remote(part, part, wz_s.at[r], wz_r.at[r], at(zl=1 - zl))

    def w_start(i):
        for j in range(3):
            w_copy(i, j).start()

    def w_wait(i):
        for j in range(3):
            w_copy(i, j).wait_recv()

    def w_rows(from_y, r):
        rows = pl.ds(core * 8 + from_y * 2, 2)
        if r is None:
            return wb.at[rows]
        return wb.at[rows, :, pl.ds(mult(blocks[r] * 768, 128), 768)]

    def wy_copy(r, s):
        part = w_rows(y, r)
        return remote(part, part, wy_s.at[r, s], wy_r.at[r, s], at(y=hop(y, (1, 3)[s])))

    def wq_copy(r):
        s = r // 2
        part = w_rows(hop(y, (3, 1)[s]), r)
        return remote(part, part, wq_s.at[r], wq_r.at[r], at(y=hop(y, (1, 3)[s])))

    def wc_copy(k):
        part = w_rows(hop(y, k), None)
        return remote(part, part, wc_s.at[k], wc_r.at[k], at(core=1 - core))

    def wy_start(r):
        wy_copy(r, 0).start()
        wy_copy(r, 1).start()

    w_local = []
    for j in range(3):
        ref, low, width = widths[j]
        src = ref.at[y, :, core, x]
        dst = wb.at[pl.ds(own_rows, 2), :, pl.ds(mult(x * 768 + low, 128), width)]
        copy = pltpu.make_async_copy(src, dst, wl_s.at[j])
        copy.start()
        w_local.append(copy)
    w_start(0)
    w_start(1)
    w_start(2)
    for copy in w_local:
        copy.wait()
    wy_start(0)

    def squares(c, total):
        piece = x_ref[:, pl.ds(mult(c * 512, 512), 512)].astype(F32)
        piece = piece * piece
        return total + (piece[:, :128] + piece[:, 128:256]) + (piece[:, 256:384] + piece[:, 384:])

    total = lax.fori_loop(0, 16, squares, jnp.zeros((128, 128), F32), unroll=4)
    mean = jnp.sum(total, axis=1, keepdims=True) * (1.0 / 8192)
    rstd = lax.rsqrt(mean + 1e-05)

    def x_to(to_x):
        def block(kappa, carry):
            c, yy, zz = kappa // 8, (kappa // 2) % 4, kappa % 2
            low = mult((yy * 4 + zz * 2 + c) * 512 + to_x * 128, 128)
            rows = x_ref[:, pl.ds(low, 128)].astype(F32)
            normed = rows * rstd * gain_ref[:, pl.ds(low, 128)]
            nt[to_x, kappa] = normed.T.astype(BF)
            return carry

        lax.fori_loop(0, 16, block, 0, unroll=4)

    def x_slot(from_x):
        return xst.at[:, :, pl.ds(mult((zh * 4 + from_x) * 128, 128), 128)]

    def x_copy(i):
        to_x = hop(x, HOPS[i])
        return remote(nt.at[to_x], x_slot(x), x_s.at[i], x_r.at[i], at(x=to_x))

    def xz_copy(i):
        from_x = x if i == 3 else hop(x, 4 - HOPS[i])
        slot = x_slot(from_x)
        return remote(nt.at[x] if i == 3 else slot, slot, xz_s.at[i], xz_r.at[i], at(zh=1 - zh))

    x_to(x)
    x_local = pltpu.make_async_copy(nt.at[x], x_slot(x), xl_s)
    x_local.start()
    xz_copy(3).start()
    for i in range(3):
        x_to(hop(x, HOPS[i]))
        x_copy(i).start()
    for i in range(3):
        w_wait(i)
        wz_copy(i + 1).start()
    for r in (1, 2):
        wz_copy(r).wait_recv()
        wy_start(r)

    lane = lax.broadcasted_iota(jnp.int32, (128, 128), 1)

    def rope(t, carry):
        block = (t % 4) * 2 + t // 4
        rows = pl.ds(mult(block * 128, 128), 128)
        place = jnp.broadcast_to(pos_ref[pl.ds(block, 1), :].astype(F32), (128, 128)).T
        angle = place * freq_ref[...]
        cosine = jnp.cos(angle)
        sine = jnp.sin(angle)
        sine = jnp.where(lane < 64, sine, -sine)
        out = pl.ds(mult(t * 128, 128), 128)
        for h in range(5):
            v = q_ref[rows, pl.ds(h * 128, 128)] if h < 4 else k_ref[rows, :]
            v = v.astype(F32)
            back = v * cosine + pltpu.roll(v, 64, 1) * sine
            cot[out, pl.ds(mult(x * 768 + h * 128, 128), 128)] = back.astype(BF)
        cot[out, pl.ds(mult(x * 768 + 640, 128), 128)] = v_ref[rows, :]
        return carry

    lax.fori_loop(0, 8, rope, 0, unroll=2)

    def low_row(h):
        return (1 - zh if h == 0 else zh) * 512

    def c_copy(h, s):
        part = cot.at[pl.ds(mult(low_row(h), 512), 512), pl.ds(mult(x * 768, 128), 768)]
        return remote(part, part, c_s.at[h, s], c_r.at[h, s], at(x=hop(x, (1, 3)[s])))

    def cq_copy(h, s):
        b = blocks[1 + s]
        part = cot.at[pl.ds(mult(low_row(h) + s * 256, 256), 256), pl.ds(mult(b * 768, 128), 768)]
        return remote(part, part, cq_s.at[h, s], cq_r.at[h, s], at(x=hop(x, (1, 3)[s])))

    wy_copy(0, 0).wait_recv()
    wq_copy(0).start()
    for i in (0, 1):
        x_copy(i).wait_recv()
        xz_copy(i).start()
    wz_copy(3).wait_recv()
    wy_start(3)
    wy_copy(1, 0).wait_recv()
    wq_copy(1).start()
    wy_copy(2, 1).wait_recv()
    wq_copy(2).start()
    x_copy(2).wait_recv()
    xz_copy(2).start()
    c_copy(0, 0).start()
    c_copy(0, 1).start()
    wc_copy(0).start()
    wy_copy(3, 1).wait_recv()
    wq_copy(3).start()
    for s in (0, 1):
        c_copy(0, s).wait_recv()
        cq_copy(0, s).start()
    for r in (0, 1, 2):
        wy_copy(r, 1 if r < 2 else 0).wait_recv()
    wy_copy(3, 0).wait_recv()
    wc_copy(3).start()
    wc_copy(1).start()
    for r in range(4):
        wq_copy(r).wait_recv()
    wc_copy(2).start()
    for s in (0, 1):
        cq_copy(0, s).wait_send()
        c_copy(1, s).start()

    def wdot(kappa, b):
        return jnp.dot(
            xst[pl.ds(kappa, 2)].reshape(256, 1024),
            cot[:, pl.ds(mult(b * 768, 128), 768)],
            preferred_element_type=F32,
        )

    def chunk_y(k):
        return hop(y, 6 - k)

    def pc_copy(r, k):
        return remote(coresend.at[r % 2, k], sum2.at[r, k], pc_s.at[r, k], pc_r.at[r, k], at(core=1 - core))

    def ph_copy(r, s):
        src = sum2.at[r, 0, pl.ds(s * 128, 128)]
        return remote(src, yrel.at[r, s], ph_s.at[r, s], ph_r.at[r, s], at(y=hop(y, (1, 3)[s])))

    def py_copy(r, s):
        src = sum2.at[r, (1, 3)[s]]
        return remote(src, yrecv.at[r, s], py_s.at[r, s], py_r.at[r, s], at(y=hop(y, (1, 3)[s])))

    def pz_copy(r):
        return remote(zlsend.at[r], zlrecv.at[r], pz_s.at[r], pz_r.at[r], at(zl=1 - zl))

    def px_copy(r):
        if r == 0:
            return pltpu.make_async_copy(xsend.at[r], dws_ref.at[x], pl_s)
        return remote(xsend.at[r], dws_ref.at[x], px_s.at[r - 1], px_r.at[r - 1], at(x=blocks[r]))

    def wother(r):
        b = blocks[r]

        def other(k, carry):
            if r >= 2:
                pc_copy(r - 2, k).wait_send()
            coresend[r % 2, k] = wdot((1 - core) * 8 + chunk_y(k) * 2, b).astype(BF)
            pc_copy(r, k).start()
            return carry

        lax.fori_loop(0, 4, other, 0)

    def wown(r):
        b = blocks[r]

        def own(k, carry):
            part = wdot(core * 8 + chunk_y(k) * 2, b)
            pc_copy(r, k).wait_recv()
            sum2[r, k] = (part + sum2[r, k].astype(F32)).astype(BF)

            @pl.when(k == 0)
            def _():
                ph_copy(r, 0).start()
                ph_copy(r, 1).start()

            return carry

        lax.fori_loop(0, 4, own, 0)

    def wpass(r):
        for s in (0, 1):
            k = (1, 3)[s]
            rows = pl.ds(s * 128, 128)
            ph_copy(r, s).wait_recv()
            sum2[r, k, rows, :] = (sum2[r, k, rows, :].astype(F32) + yrel[r, s].astype(F32)).astype(BF)
            py_copy(r, s).start()

    def y_total(r, low):
        rows = pl.ds(mult(low * 128, 128), 128)
        return sum2[r, 2, rows, :].astype(F32) + (
            yrecv[r, 0, rows, :].astype(F32) + yrecv[r, 1, rows, :].astype(F32)
        )

    def stage_a(r):
        for s in (0, 1):
            py_copy(r, s).wait_recv()
        zlsend[r] = y_total(r, 1 - zl).astype(BF)
        pz_copy(r).start()

    def stage_b(r):
        pz_copy(r).wait_recv()
        xsend[r] = (y_total(r, zl) + zlrecv[r].astype(F32)).astype(BF)
        px_copy(r).start()

    def ddot(half, n):
        return lax.dot_general(
            cot[pl.ds(mult(half * 512, 512), 512), :],
            wb[pl.ds(n * 2, 2)].reshape(256, 3072),
            (((1,), (1,)), ((), ())),
            preferred_element_type=F32,
        )

    def dz_copy(n):
        return remote(dxsend.at[n], dxrecv.at[n], dz_s.at[n], dz_r.at[n], at(zh=1 - zh))

    def da_copy(n, i):
        to_x = hop(x, HOPS[i])
        return remote(
            dxown.at[n, pl.ds(mult(to_x * 128, 128), 128)],
            dxs_ref.at[x, :, pl.ds(mult(n * 256, 256), 256)],
            da_s.at[n, i], da_r.at[n, i], at(x=to_x),
        )

    def dl_copy(n):
        return pltpu.make_async_copy(
            dxown.at[n, pl.ds(mult(x * 128, 128), 128)],
            dxs_ref.at[x, :, pl.ds(mult(n * 256, 256), 256)],
            dl_s.at[n],
        )

    def d_other(n, carry):
        dxsend[n] = ddot(1 - zh, n).astype(BF)
        dz_copy(n).start()
        return carry

    def d_own(n, carry):
        part = ddot(zh, n)
        dz_copy(n).wait_recv()
        dxown[n] = (part + dxrecv[n].astype(F32)).astype(BF)
        for i in (2, 0, 1):
            da_copy(n, i).start()
        dl_copy(n).start()
        return carry

    x_local.wait()
    for i in (3, 0, 1, 2):
        xz_copy(i).wait_recv()
    wother(0)
    wown(0)
    for s in (0, 1):
        cq_copy(0, s).wait_recv()
    for k in range(4):
        wc_copy(k).wait_recv()
    lax.fori_loop(0, 3, d_other, 0)
    wpass(0)
    lax.fori_loop(3, 8, d_other, 0)
    for s in (0, 1):
        c_copy(1, s).wait_recv()
        cq_copy(1, s).start()
    wother(1)
    wown(1)
    wother(2)
    wpass(1)
    wown(2)
    for s in (0, 1):
        cq_copy(1, s).wait_recv()
    wother(3)
    wpass(2)
    wown(3)
    lax.fori_loop(0, 2, d_own, 0)
    wpass(3)
    lax.fori_loop(2, 4, d_own, 0)
    stage_a(0)
    lax.fori_loop(4, 6, d_own, 0)
    stage_a(1)
    stage_b(0)
    stage_a(2)
    lax.fori_loop(6, 7, d_own, 0)
    stage_b(1)
    stage_b(2)
    stage_a(3)
    lax.fori_loop(7, 8, d_own, 0)
    stage_b(3)

    for i in range(3):
        for j in range(3):
            w_copy(i, j).wait_send()
        x_copy(i).wait_send()
    for r in range(4):
        if r > 0:
            wz_copy(r).wait_send()
        wy_copy(r, 0).wait_send()
        wy_copy(r, 1).wait_send()
        wq_copy(r).wait_send()
        wc_copy(r).wait_send()
        xz_copy(r).wait_send()
    for h in (0, 1):
        for s in (0, 1):
            c_copy(h, s).wait_send()
            if h == 1:
                cq_copy(h, s).wait_send()
    for r in (2, 3):
        for k in range(4):
            pc_copy(r, k).wait_send()
    for r in range(4):
        for s in (0, 1):
            ph_copy(r, s).wait_send()
            py_copy(r, s).wait_send()
        pz_copy(r).wait_send()
        px_copy(r).wait()

    def drain(n, carry):
        dz_copy(n).wait_send()
        for i in range(3):
            da_copy(n, i).wait()
        dl_copy(n).wait()
        return carry

    lax.fori_loop(0, 8, drain, 0)


def core_call(layer_input, gain, wq, wk, wv, qg, kg, vg, pos, freq):
    vm = pl.BlockSpec(memory_space=pltpu.VMEM)
    hbm = pl.BlockSpec(memory_space=pl.ANY)
    dma = pltpu.SemaphoreType.DMA
    return pl.pallas_call(
        core_kernel,
        out_shape=(
            jax.ShapeDtypeStruct((4, 128, 2048), BF),
            jax.ShapeDtypeStruct((4, 128, 768), BF),
        ),
        in_specs=[vm, vm, hbm, hbm, hbm, vm, vm, vm, vm, vm],
        out_specs=(hbm, hbm),
        scratch_shapes=[
            pltpu.VMEM((4, 16, 128, 128), BF),
            pltpu.VMEM((16, 128, 1024), BF),
            pltpu.VMEM((1024, 3072), BF),
            pltpu.VMEM((16, 128, 3072), BF),
            pltpu.VMEM((2, 4, 256, 768), BF),
            pltpu.VMEM((4, 4, 256, 768), BF),
            pltpu.VMEM((4, 2, 128, 768), BF),
            pltpu.VMEM((4, 2, 256, 768), BF),
            pltpu.VMEM((4, 128, 768), BF),
            pltpu.VMEM((4, 128, 768), BF),
            pltpu.VMEM((4, 128, 768), BF),
            pltpu.VMEM((8, 512, 256), BF),
            pltpu.VMEM((8, 512, 256), BF),
            pltpu.VMEM((8, 512, 256), BF),
            dma((3, 3)), dma((3, 3)), dma((3,)), dma((4,)), dma((4,)),
            dma((4, 2)), dma((4, 2)), dma((4,)), dma((4,)), dma((4,)), dma((4,)),
            dma((3,)), dma((3,)), dma, dma((4,)), dma((4,)),
            dma((2, 2)), dma((2, 2)), dma((2, 2)), dma((2, 2)),
            dma((4, 4)), dma((4, 4)), dma((4, 2)), dma((4, 2)), dma((4, 2)), dma((4, 2)), dma((4,)), dma((4,)),
            dma((3,)), dma((3,)), dma,
            dma((8,)), dma((8,)), dma((8, 3)), dma((8, 3)), dma((8,)),
        ],
        compiler_params=pltpu.CompilerParams(
            collective_id=1, has_side_effects=True, vmem_limit_bytes=63 * 2**20
        ),
        cost_estimate=pl.CostEstimate(flops=26 * 10**9, bytes_accessed=20 * 10**6, transcendentals=0),
        name="projection_backward",
    )(layer_input, gain, wq, wk, wv, qg, kg, vg, pos, freq)


def norm_back_kernel(x_ref, gain_ref, d_ref, s_ref, o_ref, k_ref, v_ref, q_ref):
    rows = x_ref.shape[0]
    order = [(s, kappa) for s in range(4) for kappa in range(16)]
    factor = 1.0 / math.sqrt(16384)
    q_ref[...] = s_ref[0, :, :512].astype(F32) * factor
    k_ref[...] = s_ref[0, :, 512:640].astype(F32) * factor
    v_ref[...] = s_ref[0, :, 640:].astype(F32) * factor

    def low(s, kappa):
        c, yy, zz = kappa // 8, (kappa // 2) % 4, kappa % 2
        return (yy * 4 + zz * 2 + c) * 512 + s * 128

    square = jnp.zeros((rows, 128), F32)
    cross = jnp.zeros((rows, 128), F32)
    for s, kappa in order:
        cols = pl.ds(low(s, kappa), 128)
        v = x_ref[:, cols].astype(F32)
        g = d_ref[s, :, pl.ds(kappa * 128, 128)].astype(F32) * gain_ref[:, cols]
        square = square + v * v
        cross = cross + v * g
    mean = jnp.sum(square, axis=1, keepdims=True) * (1.0 / 8192)
    rstd = lax.rsqrt(mean + 1e-05)
    dot = jnp.sum(cross, axis=1, keepdims=True) * (1.0 / 8192) * rstd
    for s, kappa in order:
        cols = pl.ds(low(s, kappa), 128)
        v = x_ref[:, cols].astype(F32)
        g = d_ref[s, :, pl.ds(kappa * 128, 128)].astype(F32) * gain_ref[:, cols]
        o_ref[:, cols] = (rstd * (g - (v * rstd) * dot)).astype(BF)


def norm_back(layer_input, gain, parts, sums):
    rows = 32

    def out(width):
        return pl.BlockSpec((128, width), lambda i: (i, 0))

    return pl.pallas_call(
        norm_back_kernel,
        out_shape=(
            jax.ShapeDtypeStruct((128, 8192), BF),
            jax.ShapeDtypeStruct((512, 128), F32),
            jax.ShapeDtypeStruct((512, 128), F32),
            jax.ShapeDtypeStruct((512, 512), F32),
        ),
        grid=(128 // rows,),
        in_specs=[
            pl.BlockSpec((rows, 8192), lambda i: (i, 0)),
            pl.BlockSpec((1, 8192), lambda i: (0, 0)),
            pl.BlockSpec((4, rows, 2048), lambda i: (0, i, 0)),
            pl.BlockSpec((1, 128, 768), lambda i: (i, 0, 0)),
        ],
        out_specs=(pl.BlockSpec((rows, 8192), lambda i: (i, 0)), out(128), out(128), out(512)),
        compiler_params=pltpu.CompilerParams(vmem_limit_bytes=63 * 2**20),
        name="norm_backward",
    )(layer_input, gain, parts, sums)


def shards(layer_input, norm_gain, wq, wk, wv, qg, kg, vg, positions):
    gain = norm_gain.reshape(1, 8192)
    parts, sums = core_call(
        layer_input,
        gain,
        wq.reshape(4, 2, 2, 4, 128, 512),
        wk.reshape(4, 2, 2, 4, 128, 128),
        wv.reshape(4, 2, 2, 4, 128, 128),
        qg, kg, vg,
        positions.reshape(8, 128),
        jnp.asarray(FREQ),
    )
    return norm_back(layer_input, gain, parts, sums)


def solution(mesh):
    in_specs = (
        P(("dp", "mp"), None),
        P(),
        P(None, "mp"),
        P(None, "mp"),
        P(None, "mp"),
        P("dp", "mp"),
        P("dp", "mp"),
        P("dp", "mp"),
        P("dp"),
    )
    out_specs = (P(("dp", "mp"), None), P("dp", "mp"), P("dp", "mp"), P("dp", "mp"))
    return jax.shard_map(shards, mesh=mesh, in_specs=in_specs, out_specs=out_specs, check_vma=False)
```
